256 devices in a mesh: grp: 8 (over z_lo, core), dev: 32 (over y, x, z_hi).
Axes of the slice: x: 4, y: 4, z: 8 (z_hi: 2, z_lo: 4; z = z_hi * 4 + z_lo), core: 2. Of those that a mesh axis runs over, the one named last changes fastest.
Arguments:
- spectra: bfloat16 [4096, 16, 256], P(('grp', 'dev')), may hold values from -6 to 6
- round_mask: int32 [1], replicated, may hold values from 0 to 32767
Outputs:
- correlations: bfloat16 [768, 4096, 512], P(None, ('grp', 'dev'))
The draws below stay inside these ranges and needn't reach their ends.
All inputs are finite; a program needn't handle non-finite values.
Results may differ from the reference program's by a relative error of at most 0.0056.
Values may be sent and summed in bfloat16 or wider, within the bound.
A program may use at most 128 MiB of HBM per device.

```python
import math
import jax
import jax.numpy as jnp
from jax import lax

NF = 256
WINDOWS = 8
LAGS = 768
FREQ_LO = 64
NFFT = 1024
GROUP_CH = 512
CHANNELS = 4096
N_GRP = 8


def level_of(own_key, shape, pieces, smallest, top_value):
    def one(position, blocks):
        draws = jax.random.uniform(jax.random.fold_in(jax.random.fold_in(own_key, 6), position), (blocks,), jnp.float32, smallest / len(pieces), top_value / len(pieces))
        return jnp.repeat(jnp.exp(draws), shape[position] // blocks).reshape((-1,) + (1,) * (len(shape) - position - 1))

    factor_of = one(*pieces[0])
    for cut in pieces[1:]:
        factor_of = factor_of * one(*cut)
    return factor_of


def noise(own_key, extent, scale, bound, shards=(), kind=jnp.bfloat16):
    result = scale * jax.random.normal(own_key, extent, jnp.float32)
    if shards:
        result = result * level_of(own_key, extent, shards, -0.22, 0.18)
    return jnp.clip(result, -bound, bound).astype(kind)


def setup_inputs(seed: int = 0) -> dict:
    streams_of = jax.random.split(jax.random.key(seed), 3)
    spectra = noise(streams_of[0], (CHANNELS, 2 * WINDOWS, NF), 1.0, 6.0, ((0, 256),))
    round_mask = jax.random.randint(streams_of[1], (1,), 0, 4096 * N_GRP).astype(jnp.int32)
    return {"spectra": spectra, "round_mask": round_mask}


def make_table():
    freq = jnp.arange(NF, dtype=jnp.int32)
    lag = jnp.arange(LAGS, dtype=jnp.int32) - LAGS // 2
    steps = jnp.mod((FREQ_LO + freq)[:, None] * lag[None, :], NFFT)
    theta = 2.0 * math.pi / NFFT * steps.astype(jnp.float32)
    taper = 0.5 - 0.5 * jnp.cos(2.0 * math.pi * (freq.astype(jnp.float32) + 0.5) / NF)
    taper = taper / math.sqrt(2.0 * WINDOWS * NF)
    table = jnp.stack([taper[:, None] * jnp.cos(theta), -taper[:, None] * jnp.sin(theta)], axis=1)
    return table.astype(jnp.bfloat16)

def reference(spectra, round_mask):
    table = make_table().astype(jnp.float32)
    block = min(8, NF)
    blocks = NF // block
    mask = jnp.mod(round_mask[0], N_GRP).astype(jnp.int32)

    def one_group(group):
        partner = jnp.bitwise_xor(group, mask)
        own = lax.dynamic_slice_in_dim(spectra, (group * GROUP_CH).astype(jnp.int32), GROUP_CH, 0).astype(jnp.float32)
        other = lax.dynamic_slice_in_dim(spectra, (partner * GROUP_CH).astype(jnp.int32), GROUP_CH, 0).astype(jnp.float32)
        rotated = jnp.concatenate([own[:, WINDOWS:], -own[:, :WINDOWS]], axis=1)
        stacked = jnp.concatenate([own, rotated], axis=0)

        def add_block(total, index):
            first = (index * block).astype(jnp.int32)
            left = lax.dynamic_slice_in_dim(stacked, first, block, 2)
            right = lax.dynamic_slice_in_dim(other, first, block, 2)
            cross = jnp.einsum('cwk,pwk->kcp', left, right)
            cross = lax.optimization_barrier(cross.astype(jnp.bfloat16)).astype(jnp.float32)
            cross = cross.reshape(block, 2, GROUP_CH, GROUP_CH)
            weights = lax.dynamic_slice_in_dim(table, first, block, 0)
            return (total + jnp.einsum('krl,krcp->lcp', weights, cross), None)
        start = jnp.zeros((LAGS, GROUP_CH, GROUP_CH), jnp.float32)
        total, _ = lax.scan(add_block, start, jnp.arange(blocks, dtype=jnp.int32))
        return total.astype(jnp.bfloat16)
    groups = lax.map(one_group, jnp.arange(N_GRP, dtype=jnp.int32))
    return jnp.transpose(groups, (1, 0, 2, 3)).reshape(LAGS, CHANNELS, GROUP_CH)
```

```python
import functools
import math

import jax
import jax.numpy as jnp
import numpy as np
from jax import lax
from jax.experimental import pallas as pl
from jax.experimental.pallas import tpu as pltpu
from jax.sharding import PartitionSpec as P

MESH = pl.DeviceIdType.MESH
NF = 256
WINDOWS = 8
LAGS = 768
HALF = LAGS // 2
FREQ_LO = 64
NFFT = 1024
ROWS = 400
CH = 16
F32, BF16 = jnp.float32, jnp.bfloat16


def make_tables():
    freq = np.arange(NF)
    steps = ((FREQ_LO + freq)[None, :] * np.arange(ROWS)[:, None]) % NFFT
    theta = 2.0 * math.pi / NFFT * steps
    taper = (0.5 - 0.5 * np.cos(2.0 * math.pi * (freq + 0.5) / NF)) / math.sqrt(2.0 * WINDOWS * NF)
    return (taper * np.cos(theta)).astype(jnp.bfloat16), (-taper * np.sin(theta)).astype(jnp.bfloat16)


def prepare(x_ref, xs, send):
    for half in range(2):
        xs[half] = x_ref[:, :, half * 128 : half * 128 + 128].reshape(256, 128).astype(F32)
    lane = lax.broadcasted_iota(jnp.int32, (CH, 128), 1) // 16
    for half in range(2):
        for h in range(2):
            rows = [xs[half, pl.ds(8 * h + w, CH, stride=16), :] for w in range(8)]
            for g in range(8):
                acc = None
                for w in range(8):
                    shift = ((w - g) * 16) % 128
                    v = rows[w] if shift == 0 else pltpu.roll(rows[w], shift, 1)
                    acc = v if acc is None else jnp.where(lane == w, v, acc)
                first = g * 256 + h * 128
                send[half, :, first : first + 128] = acc.astype(BF16)


def build_diag(send, diag):
    mask = (lax.broadcasted_iota(jnp.int32, (16, 128), 1) % 16) == lax.broadcasted_iota(jnp.int32, (16, 128), 0)
    for half in range(2):

        def body(g, carry):
            base = pl.multiple_of(g * 256, 256)
            lo = send[half, :, pl.ds(base, 128)].astype(F32)
            hi = send[half, :, pl.ds(base + 128, 128)].astype(F32)
            for c in range(CH):
                re = jnp.where(mask, jnp.broadcast_to(lo[c : c + 1], (16, 128)), 0.0)
                im = jnp.where(mask, jnp.broadcast_to(hi[c : c + 1], (16, 128)), 0.0)
                r0 = c * 32
                diag[half * 8 + g, r0 : r0 + 16, 0:128] = re.astype(BF16)
                diag[half * 8 + g, r0 : r0 + 16, 128:256] = im.astype(BF16)
                diag[half * 8 + g, r0 + 16 : r0 + 32, 0:128] = im.astype(BF16)
                diag[half * 8 + g, r0 + 16 : r0 + 32, 128:256] = (-re).astype(BF16)
            return carry

        lax.fori_loop(0, 8, body, 0)


def cross_half(whole, diag, cross, row, half):
    def body(g, carry):
        right = whole[half, pl.ds(row, 128), pl.ds(pl.multiple_of(g * 256, 256), 256)]
        gg = half * 8 + g
        k0 = pl.multiple_of(gg * 16, 16)
        res = lax.dot_general(diag[gg], right, (((1,), (1,)), ((), ())), preferred_element_type=F32).astype(BF16)
        for c in range(CH):
            for r in range(2):
                r0 = c * 32 + r * 16
                cross[r, c // 2, pl.ds(k0, 16), (c % 2) * 128 : (c % 2) * 128 + 128] = res[r0 : r0 + 16]
        return carry

    lax.fori_loop(0, 8, body, 0, unroll=4)


def lags_of(tc, ts, cross, scr):
    def body(cp, carry):
        even = jnp.dot(tc[...], cross[0, cp], preferred_element_type=F32)
        odd = jnp.dot(ts[...], cross[1, cp], preferred_element_type=F32)
        later, earlier = even + odd, even - odd
        for b in range(2):
            scr[0, pl.ds(2 * cp + b, ROWS, stride=CH), :] = later[:, b * 128 : b * 128 + 128]
            scr[1, pl.ds(2 * cp + b, ROWS, stride=CH), :] = earlier[:, b * 128 : b * 128 + 128]
        return carry

    lax.fori_loop(0, 8, body, 0, unroll=2)


def finish(scr, out):
    def body(i, carry):
        for u in range(8):
            d = i * 8 + u
            out[HALF + d] = scr[0, pl.ds(pl.multiple_of(d * CH, CH), CH), :].astype(BF16)
            out[HALF - 1 - d] = scr[1, pl.ds(pl.multiple_of(d * CH + CH, CH), CH), :].astype(BF16)
        return carry

    lax.fori_loop(0, HALF // 8, body, 0)


def flip(z_lo, bits):
    if bits & 1:
        z_lo = z_lo + 1 - 2 * lax.rem(z_lo, 2)
    if bits & 2:
        z_lo = lax.rem(z_lo + 2, 4)
    return z_lo


OFFSETS = (0, -1, 1, 2)


def parts_of(half, dx, dy):
    first, second = (dx, dy) if half == 0 else (dy, dx)
    if second == 2 or (second == 0 and first == 2):
        return ("a", "b")
    return ("ab",)


KEYS = {}
for _half in range(2):
    for _dx in OFFSETS:
        for _dy in OFFSETS:
            if (_dx, _dy) != (0, 0):
                for _part in parts_of(_half, _dx, _dy):
                    KEYS[_half, _dx, _dy, _part] = len(KEYS)
for _half in range(2):
    for _side in range(2):
        KEYS["z", _half, _side] = len(KEYS)


def wrap(offset):
    offset %= 4
    return offset - 4 if offset == 3 else offset


def gather_kernel(code, x_ref, tc, ts, tiles, last, xs, send, diag, whole, cross, scr, send_sem, recv_sem):
    grp, dev = lax.axis_index("grp"), lax.axis_index("dev")
    z_lo, core = grp // 2, lax.rem(grp, 2)
    y, x, z_hi = dev // 8, lax.rem(dev // 2, 4), lax.rem(dev, 2)

    def at(off_x, off_y):
        return grp, lax.rem(y + off_y + 4, 4) * 8 + lax.rem(x + off_x + 4, 4) * 2 + z_hi

    pair = flip(z_lo, code >> 1) * 2 + (1 - core if code & 1 else core)
    other = dev + 1 - 2 * z_hi
    sides = [(pair, dev), (pair, other)]
    if code == 0:
        sides[0] = None
    steps = {("x", 1): at(1, 0), ("x", -1): at(-1, 0), ("y", 1): at(0, 1), ("y", -1): at(0, -1)}

    barrier = pltpu.get_barrier_semaphore()
    greet = [s for s in sides if s is not None] + list(steps.values())
    for device in greet:
        pl.semaphore_signal(barrier, inc=1, device_id=device, device_id_type=MESH)

    prepare(x_ref, xs, send)
    pl.semaphore_wait(barrier, len(greet))

    started = []

    def z_copy(half, side):
        k = KEYS["z", half, side]
        own = whole.at[half, pl.ds(pl.multiple_of(dev * 16, 16), 16), :]
        return pltpu.make_async_remote_copy(
            src_ref=send.at[half], dst_ref=own, send_sem=send_sem.at[k], recv_sem=recv_sem.at[k],
            device_id=sides[side], device_id_type=MESH,
        )

    def z_arrive(half, side):
        k = KEYS["z", half, side]
        row = dev if side == 0 else other
        land = whole.at[half, pl.ds(pl.multiple_of(row * 16, 16), 16), :]
        pltpu.make_async_remote_copy(
            src_ref=send.at[half], dst_ref=land, send_sem=send_sem.at[k], recv_sem=recv_sem.at[k],
            device_id=sides[side], device_id_type=MESH,
        ).wait_recv()

    def block(half, dx, dy, part):
        row = (lax.rem(y + dy + 4, 4) * 8 + lax.rem(x + dx + 4, 4) * 2) * 16
        if part == "ab":
            return whole.at[half, pl.ds(pl.multiple_of(row, 32), 32), :]
        return whole.at[half, pl.ds(pl.multiple_of(row + (16 if part == "b" else 0), 16), 16), :]

    def copy(half, dx, dy, part, k, device):
        ref = block(half, dx, dy, part)
        return pltpu.make_async_remote_copy(
            src_ref=ref, dst_ref=ref, send_sem=send_sem.at[k], recv_sem=recv_sem.at[k],
            device_id=device, device_id_type=MESH,
        )

    def push(half, dx, dy, part, axis, way):
        to = (wrap(dx - way), dy) if axis == "x" else (dx, wrap(dy - way))
        c = copy(half, dx, dy, part, KEYS[half, to[0], to[1], part], steps[axis, way])
        c.start()
        started.append(c)

    def arrive(half, dx, dy):
        for part in parts_of(half, dx, dy):
            copy(half, dx, dy, part, KEYS[half, dx, dy, part], steps["x", 1]).wait_recv()

    axes = (("x", "y"), ("y", "x"))

    def swap(half, a, b):
        return (a, b) if half == 0 else (b, a)

    def send_full(half, a, b, which):
        dx, dy = swap(half, a, b)
        for way in (1, -1):
            push(half, dx, dy, "ab", axes[half][which], way)

    def forward(half, a, b, which):
        dx, dy = swap(half, a, b)
        came = (a, b)[which]
        push(half, dx, dy, "a" if came == -1 else "b", axes[half][which], -came)

    def take(half, a, b):
        arrive(half, *swap(half, a, b))

    for half in range(2):
        for side in range(2):
            if sides[side] is not None:
                c = z_copy(half, side)
                c.start()
                started.append(c)
    if code == 0:
        for half in range(2):
            whole[half, pl.ds(pl.multiple_of(dev * 16, 16), 16), :] = send[half]
    build_diag(send, diag)

    for half in range(2):
        for side in range(2):
            if sides[side] is not None:
                z_arrive(half, side)
        send_full(half, 0, 0, 0)
        send_full(half, 0, 0, 1)
    for half in range(2):
        for a in (-1, 1):
            take(half, a, 0)
            forward(half, a, 0, 0)
            send_full(half, a, 0, 1)
    for half in range(2):
        for b in (-1, 1):
            take(half, 0, b)
            forward(half, 0, b, 1)
    for half in range(2):
        take(half, 2, 0)
        send_full(half, 2, 0, 1)

    def row_of(dy):
        return pl.multiple_of(lax.rem(y + dy + 4, 4) * 128, 128)

    cross_half(whole, diag, cross, row_of(0), 0)
    for half in range(2):
        for a in (-1, 1):
            for b in (-1, 1):
                take(half, a, b)
                forward(half, a, b, 1)
    arrive(1, 2, 0)
    cross_half(whole, diag, cross, row_of(0), 1)
    lags_of(tc, ts, cross, scr)
    for half in range(2):
        for b in (-1, 1):
            take(half, 2, b)
            forward(half, 2, b, 1)
    finish(scr, tiles.at[0])
    for i, dy in enumerate((-1, 1)):
        cross_half(whole, diag, cross, row_of(dy), 0)
        arrive(1, 2, dy)
        cross_half(whole, diag, cross, row_of(dy), 1)
        lags_of(tc, ts, cross, scr)
        finish(scr, tiles.at[1 + i])
    for dx in OFFSETS:
        arrive(0, dx, 2)
    cross_half(whole, diag, last, row_of(2), 0)
    arrive(1, 2, 2)
    cross_half(whole, diag, last, row_of(2), 1)
    for c in started:
        c.wait_send()


def write_kernel(tiles, last, tc, ts, out, scr, stage, sem):
    y = lax.axis_index("dev") // 8

    def put(src, dy, k):
        lanes = pl.multiple_of(lax.rem(y + dy + 4, 4) * 128, 128)
        return pltpu.make_async_copy(src, out.at[:, :, pl.ds(lanes, 128)], sem.at[k])

    copies = [put(tiles.at[i], dy, i) for i, dy in enumerate((0, -1, 1))]
    for c in copies:
        c.start()
    lags_of(tc, ts, last, scr)
    finish(scr, stage)
    copies.append(put(stage, 2, 3))
    copies[-1].start()
    for c in copies:
        c.wait()


def on_device(spectra, round_mask):
    mask = jnp.mod(round_mask[0], lax.axis_size("grp"))
    tc, ts = (jnp.asarray(t) for t in make_tables())
    vmem = pl.BlockSpec(memory_space=pltpu.VMEM)

    def gather(code, block, cos, sin):
        return pl.pallas_call(
            functools.partial(gather_kernel, code),
            out_shape=(
                jax.ShapeDtypeStruct((3, LAGS, CH, 128), BF16),
                jax.ShapeDtypeStruct((2, 8, NF, 256), BF16),
            ),
            in_specs=[vmem] * 3,
            out_specs=(vmem, vmem),
            scratch_shapes=[
                pltpu.VMEM((2, 256, 128), F32),
                pltpu.VMEM((2, CH, 2048), BF16),
                pltpu.VMEM((16, 512, 256), BF16),
                pltpu.VMEM((2, 512, 2048), BF16),
                pltpu.VMEM((2, 8, NF, 256), BF16),
                pltpu.VMEM((2, ROWS * CH, 128), F32),
                pltpu.SemaphoreType.DMA((len(KEYS),)),
                pltpu.SemaphoreType.DMA((len(KEYS),)),
            ],
            compiler_params=pltpu.CompilerParams(
                collective_id=code, has_side_effects=True, vmem_limit_bytes=36 * 2**20
            ),
            name=f"gather_{code}",
        )(block, cos, sin)

    tiles, last = lax.switch(mask, [functools.partial(gather, code) for code in range(8)], spectra, tc, ts)
    return pl.pallas_call(
        write_kernel,
        out_shape=jax.ShapeDtypeStruct((LAGS, CH, 512), BF16),
        in_specs=[vmem] * 4,
        out_specs=pl.BlockSpec(memory_space=pl.ANY),
        scratch_shapes=[
            pltpu.VMEM((2, ROWS * CH, 128), F32),
            pltpu.VMEM((LAGS, CH, 128), BF16),
            pltpu.SemaphoreType.DMA((4,)),
        ],
        compiler_params=pltpu.CompilerParams(vmem_limit_bytes=36 * 2**20),
        name="write",
    )(tiles, last, tc, ts)


def solution(mesh):
    return jax.shard_map(
        on_device,
        mesh=mesh,
        in_specs=(P(("grp", "dev"), None, None), P()),
        out_specs=P(None, ("grp", "dev"), None),
        check_vma=False,
    )
```

```python
import functools
import math

import jax
import jax.numpy as jnp
import numpy as np
from jax import lax
from jax.experimental import pallas as pl
from jax.experimental.pallas import tpu as pltpu
from jax.sharding import PartitionSpec as P

MESH = pl.DeviceIdType.MESH
NF = 256
WINDOWS = 8
LAGS = 768
HALF = LAGS // 2
FREQ_LO = 64
NFFT = 1024
ROWS = 400
CH = 16
PIECES = 4
F32, BF16 = jnp.float32, jnp.bfloat16


def make_tables():
    freq = np.arange(NF)
    steps = ((FREQ_LO + freq)[None, :] * np.arange(ROWS)[:, None]) % NFFT
    theta = 2.0 * math.pi / NFFT * steps
    taper = (0.5 - 0.5 * np.cos(2.0 * math.pi * (freq + 0.5) / NF)) / math.sqrt(2.0 * WINDOWS * NF)
    return np.stack([taper * np.cos(theta), -taper * np.sin(theta)]).astype(jnp.bfloat16)


def prepare(x_ref, xs, send):
    for half in range(2):
        xs[half] = x_ref[:, :, half * 128 : half * 128 + 128].reshape(256, 128).astype(F32)
    lane = lax.broadcasted_iota(jnp.int32, (CH, 128), 1) // 16
    for half in range(2):
        for h in range(2):
            rows = [xs[half, pl.ds(8 * h + w, CH, stride=16), :] for w in range(8)]
            for g in range(8):
                acc = None
                for w in range(8):
                    shift = ((w - g) * 16) % 128
                    v = rows[w] if shift == 0 else pltpu.roll(rows[w], shift, 1)
                    acc = v if acc is None else jnp.where(lane == w, v, acc)
                first = g * 256 + h * 128
                send[half, :, first : first + 128] = acc.astype(BF16)


def build_diag(send, diag):
    mask = (lax.broadcasted_iota(jnp.int32, (16, 128), 1) % 16) == lax.broadcasted_iota(jnp.int32, (16, 128), 0)
    for half in range(2):

        def body(g, carry):
            base = pl.multiple_of(g * 256, 256)
            lo = send[half, :, pl.ds(base, 128)].astype(F32)
            hi = send[half, :, pl.ds(base + 128, 128)].astype(F32)
            for c in range(CH):
                re = jnp.where(mask, jnp.broadcast_to(lo[c : c + 1], (16, 128)), 0.0)
                im = jnp.where(mask, jnp.broadcast_to(hi[c : c + 1], (16, 128)), 0.0)
                r0 = c * 32
                diag[half * 8 + g, r0 : r0 + 16, 0:128] = re.astype(BF16)
                diag[half * 8 + g, r0 : r0 + 16, 128:256] = im.astype(BF16)
                diag[half * 8 + g, r0 + 16 : r0 + 32, 0:128] = im.astype(BF16)
                diag[half * 8 + g, r0 + 16 : r0 + 32, 128:256] = (-re).astype(BF16)
            return carry

        lax.fori_loop(0, 8, body, 0)


def cross_half(whole, diag, cross, row, half):
    def body(g, carry):
        right = whole[half, pl.ds(row, 128), pl.ds(pl.multiple_of(g * 256, 256), 256)]
        gg = half * 8 + g
        k0 = pl.multiple_of(gg * 16, 16)
        res = lax.dot_general(diag[gg], right, (((1,), (1,)), ((), ())), preferred_element_type=F32).astype(BF16)
        for c in range(CH):
            for r in range(2):
                r0 = c * 32 + r * 16
                cross[r, c // 2, pl.ds(k0, 16), (c % 2) * 128 : (c % 2) * 128 + 128] = res[r0 : r0 + 16]
        return carry

    lax.fori_loop(0, 8, body, 0, unroll=4)


def lags_of(table, cross, scr):
    def body(cp, carry):
        even = jnp.dot(table[0], cross[0, cp], preferred_element_type=F32)
        odd = jnp.dot(table[1], cross[1, cp], preferred_element_type=F32)
        later, earlier = even + odd, even - odd
        for b in range(2):
            scr[0, pl.ds(2 * cp + b, ROWS, stride=CH), :] = later[:, b * 128 : b * 128 + 128]
            scr[1, pl.ds(2 * cp + b, ROWS, stride=CH), :] = earlier[:, b * 128 : b * 128 + 128]
        return carry

    lax.fori_loop(0, 8, body, 0, unroll=2)


def finish(scr, out):
    def body(i, carry):
        for u in range(8):
            d = i * 8 + u
            out[HALF + d] = scr[0, pl.ds(pl.multiple_of(d * CH, CH), CH), :].astype(BF16)
            out[HALF - 1 - d] = scr[1, pl.ds(pl.multiple_of(d * CH + CH, CH), CH), :].astype(BF16)
        return carry

    lax.fori_loop(0, HALF // 8, body, 0)


def flip(z_lo, bits):
    if bits & 1:
        z_lo = z_lo + 1 - 2 * lax.rem(z_lo, 2)
    if bits & 2:
        z_lo = lax.rem(z_lo + 2, 4)
    return z_lo


OFFSETS = (0, -1, 1, 2)


def parts_of(half, dx, dy):
    first, second = (dx, dy) if half == 0 else (dy, dx)
    if second == 2 or (second == 0 and first == 2):
        return ("a", "b")
    return ("ab",)


KEYS = {}
for _half in range(2):
    for _dx in OFFSETS:
        for _dy in OFFSETS:
            if (_dx, _dy) != (0, 0):
                for _part in parts_of(_half, _dx, _dy):
                    KEYS[_half, _dx, _dy, _part] = len(KEYS)

def wrap(offset):
    offset %= 4
    return offset - 4 if offset == 3 else offset


def swap_kernel(code, x_ref, own, pair, xs, land, send_sem, recv_sem):
    grp, dev = lax.axis_index("grp"), lax.axis_index("dev")
    z_lo, core, z_hi = grp // 2, lax.rem(grp, 2), lax.rem(dev, 2)
    partner = flip(z_lo, code >> 1) * 2 + (1 - core if code & 1 else core)
    sides = [(partner, dev), (partner, dev + 1 - 2 * z_hi)]
    active = [1] if code == 0 else [0, 1]

    barrier = pltpu.get_barrier_semaphore()
    for side in active:
        pl.semaphore_signal(barrier, inc=1, device_id=sides[side], device_id_type=MESH)
    prepare(x_ref, xs, own)
    pl.semaphore_wait(barrier, len(active))

    copies = []
    for half in range(2):
        for side in active:
            k = half * 2 + side
            copies.append(pltpu.make_async_remote_copy(
                src_ref=own.at[half], dst_ref=land.at[side, half], send_sem=send_sem.at[k], recv_sem=recv_sem.at[k],
                device_id=sides[side], device_id_type=MESH,
            ))
            copies[-1].start()
    same = pl.multiple_of(z_hi * 16, 16)
    far = pl.multiple_of(16 - z_hi * 16, 16)
    if code == 0:
        for half in range(2):
            pair[half, pl.ds(same, 16), :] = own[half]
    for c in copies:
        c.wait()
    for half in range(2):
        for side in active:
            pair[half, pl.ds(same if side == 0 else far, 16), :] = land[side, half]


def gather_kernel(own, pair, table_hbm, tiles, last, table, diag, whole, cross, scr, send_sem, recv_sem, table_sem):
    grp, dev = lax.axis_index("grp"), lax.axis_index("dev")
    y, x, z_hi = dev // 8, lax.rem(dev // 2, 4), lax.rem(dev, 2)

    def at(off_x, off_y):
        return grp, lax.rem(y + off_y + 4, 4) * 8 + lax.rem(x + off_x + 4, 4) * 2 + z_hi

    steps = {("x", 1): at(1, 0), ("x", -1): at(-1, 0), ("y", 1): at(0, 1), ("y", -1): at(0, -1)}
    fetch = pltpu.make_async_copy(table_hbm, table, table_sem)
    fetch.start()
    barrier = pltpu.get_barrier_semaphore()
    for device in steps.values():
        pl.semaphore_signal(barrier, inc=1, device_id=device, device_id_type=MESH)
    for half in range(2):
        whole[half, pl.ds(pl.multiple_of((y * 8 + x * 2) * 16, 32), 32), :] = pair[half]
    pl.semaphore_wait(barrier, 4)

    started = []

    def block(half, dx, dy, part):
        row = (lax.rem(y + dy + 4, 4) * 8 + lax.rem(x + dx + 4, 4) * 2) * 16
        if part == "ab":
            return whole.at[half, pl.ds(pl.multiple_of(row, 32), 32), :]
        return whole.at[half, pl.ds(pl.multiple_of(row + (16 if part == "b" else 0), 16), 16), :]

    def copy(half, dx, dy, part, k, device):
        ref = block(half, dx, dy, part)
        return pltpu.make_async_remote_copy(
            src_ref=ref, dst_ref=ref, send_sem=send_sem.at[k], recv_sem=recv_sem.at[k],
            device_id=device, device_id_type=MESH,
        )

    def push(half, dx, dy, part, axis, way):
        to = (wrap(dx - way), dy) if axis == "x" else (dx, wrap(dy - way))
        c = copy(half, dx, dy, part, KEYS[half, to[0], to[1], part], steps[axis, way])
        c.start()
        started.append(c)

    def arrive(half, dx, dy):
        for part in parts_of(half, dx, dy):
            copy(half, dx, dy, part, KEYS[half, dx, dy, part], steps["x", 1]).wait_recv()

    axes = (("x", "y"), ("y", "x"))

    def swap(half, a, b):
        return (a, b) if half == 0 else (b, a)

    def send_full(half, a, b, which):
        dx, dy = swap(half, a, b)
        for way in (1, -1):
            push(half, dx, dy, "ab", axes[half][which], way)

    def forward(half, a, b, which):
        dx, dy = swap(half, a, b)
        came = (a, b)[which]
        push(half, dx, dy, "a" if came == -1 else "b", axes[half][which], -came)

    def take(half, a, b):
        arrive(half, *swap(half, a, b))

    for half in range(2):
        send_full(half, 0, 0, 0)
        send_full(half, 0, 0, 1)
    build_diag(own, diag)
    for half in range(2):
        for a in (-1, 1):
            take(half, a, 0)
            forward(half, a, 0, 0)
            send_full(half, a, 0, 1)
    for half in range(2):
        for b in (-1, 1):
            take(half, 0, b)
            forward(half, 0, b, 1)
    for half in range(2):
        take(half, 2, 0)
        send_full(half, 2, 0, 1)

    def row_of(dy):
        return pl.multiple_of(lax.rem(y + dy + 4, 4) * 128, 128)

    fetch.wait()
    cross_half(whole, diag, cross, row_of(0), 0)
    for half in range(2):
        for a in (-1, 1):
            for b in (-1, 1):
                take(half, a, b)
                forward(half, a, b, 1)
    arrive(1, 2, 0)
    cross_half(whole, diag, cross, row_of(0), 1)
    lags_of(table, cross, scr)
    for half in range(2):
        for b in (-1, 1):
            take(half, 2, b)
            forward(half, 2, b, 1)
    finish(scr, tiles.at[0])
    for i, dy in enumerate((-1, 1)):
        cross_half(whole, diag, cross, row_of(dy), 0)
        arrive(1, 2, dy)
        cross_half(whole, diag, cross, row_of(dy), 1)
        lags_of(table, cross, scr)
        finish(scr, tiles.at[1 + i])
    for dx in OFFSETS:
        arrive(0, dx, 2)
    cross_half(whole, diag, last, row_of(2), 0)
    arrive(1, 2, 2)
    cross_half(whole, diag, last, row_of(2), 1)
    for c in started:
        c.wait_send()


def write_kernel(tiles, last, table, out, scr, stage, sem):
    y = lax.axis_index("dev") // 8

    def put(src, dy, k):
        lanes = pl.multiple_of(lax.rem(y + dy + 4, 4) * 128, 128)
        part = LAGS // PIECES
        return [
            pltpu.make_async_copy(
                src.at[pl.ds(i * part, part)], out.at[pl.ds(i * part, part), :, pl.ds(lanes, 128)], sem.at[k * PIECES + i]
            )
            for i in range(PIECES)
        ]

    copies = []
    for i, dy in enumerate((0, -1, 1)):
        copies += put(tiles.at[i], dy, i)
    for c in copies:
        c.start()
    lags_of(table, last, scr)
    finish(scr, stage)
    final = put(stage, 2, 3)
    for c in final:
        c.start()
    for c in copies + final:
        c.wait()


def on_device(spectra, round_mask):
    mask = jnp.mod(round_mask[0], lax.axis_size("grp"))
    table = jnp.asarray(make_tables())
    vmem = pl.BlockSpec(memory_space=pltpu.VMEM)

    def swap(code, block):
        return pl.pallas_call(
            functools.partial(swap_kernel, code),
            out_shape=(pltpu.VMEM((2, CH, 2048), BF16), pltpu.VMEM((2, 2 * CH, 2048), BF16)),
            in_specs=[vmem],
            out_specs=(vmem, vmem),
            scratch_shapes=[
                pltpu.VMEM((2, 256, 128), F32),
                pltpu.VMEM((2, 2, CH, 2048), BF16),
                pltpu.SemaphoreType.DMA((4,)),
                pltpu.SemaphoreType.DMA((4,)),
            ],
            compiler_params=pltpu.CompilerParams(
                collective_id=code, has_side_effects=True, vmem_limit_bytes=8 * 2**20
            ),
            name=f"swap_{code}",
        )(block)

    own, pair = lax.switch(mask, [functools.partial(swap, code) for code in range(8)], spectra)
    tiles, last, table = pl.pallas_call(
        gather_kernel,
        out_shape=(
            pltpu.VMEM((3, LAGS, CH, 128), BF16),
            pltpu.VMEM((2, 8, NF, 256), BF16),
            pltpu.VMEM((2, ROWS, NF), BF16),
        ),
        in_specs=[vmem, vmem, pl.BlockSpec(memory_space=pltpu.HBM)],
        out_specs=(vmem, vmem, vmem),
        scratch_shapes=[
            pltpu.VMEM((16, 512, 256), BF16),
            pltpu.VMEM((2, 512, 2048), BF16),
            pltpu.VMEM((2, 8, NF, 256), BF16),
            pltpu.VMEM((2, ROWS * CH, 128), F32),
            pltpu.SemaphoreType.DMA((len(KEYS),)),
            pltpu.SemaphoreType.DMA((len(KEYS),)),
            pltpu.SemaphoreType.DMA,
        ],
        compiler_params=pltpu.CompilerParams(collective_id=8, has_side_effects=True, vmem_limit_bytes=24 * 2**20),
        name="gather",
    )(own, pair, table)
    return pl.pallas_call(
        write_kernel,
        out_shape=jax.ShapeDtypeStruct((LAGS, CH, 512), BF16),
        in_specs=[vmem] * 3,
        out_specs=pl.BlockSpec(memory_space=pl.ANY),
        scratch_shapes=[
            pltpu.VMEM((2, ROWS * CH, 128), F32),
            pltpu.VMEM((LAGS, CH, 128), BF16),
            pltpu.SemaphoreType.DMA((4 * PIECES,)),
        ],
        compiler_params=pltpu.CompilerParams(vmem_limit_bytes=24 * 2**20),
        name="write",
    )(tiles, last, table)


def solution(mesh):
    return jax.shard_map(
        on_device,
        mesh=mesh,
        in_specs=(P(("grp", "dev"), None, None), P()),
        out_specs=P(None, ("grp", "dev"), None),
        check_vma=False,
    )
```

```python
import functools
import math

import jax
import jax.numpy as jnp
import numpy as np
from jax import lax
from jax.experimental import pallas as pl
from jax.experimental.pallas import tpu as pltpu
from jax.sharding import PartitionSpec as P

MESH = pl.DeviceIdType.MESH
NF = 256
WINDOWS = 8
LAGS = 768
HALF = LAGS // 2
FREQ_LO = 64
NFFT = 1024
ROWS = 400
CH = 16
PIECES = 4
F32, BF16 = jnp.float32, jnp.bfloat16


def make_tables():
    freq = np.arange(NF)
    steps = ((FREQ_LO + freq)[None, :] * np.arange(ROWS)[:, None]) % NFFT
    theta = 2.0 * math.pi / NFFT * steps
    taper = (0.5 - 0.5 * np.cos(2.0 * math.pi * (freq + 0.5) / NF)) / math.sqrt(2.0 * WINDOWS * NF)
    return np.stack([taper * np.cos(theta), -taper * np.sin(theta)]).astype(jnp.bfloat16)


def prepare(x_ref, xs, send):
    for half in range(2):
        xs[half] = x_ref[:, :, half * 128 : half * 128 + 128].reshape(256, 128).astype(F32)
    lane = lax.broadcasted_iota(jnp.int32, (CH, 128), 1) // 16
    for half in range(2):
        for h in range(2):
            rows = [xs[half, pl.ds(8 * h + w, CH, stride=16), :] for w in range(8)]
            for g in range(8):
                acc = None
                for w in range(8):
                    shift = ((w - g) * 16) % 128
                    v = rows[w] if shift == 0 else pltpu.roll(rows[w], shift, 1)
                    acc = v if acc is None else jnp.where(lane == w, v, acc)
                first = g * 256 + h * 128
                send[half, :, first : first + 128] = acc.astype(BF16)


def build_diag(send, diag):
    mask = (lax.broadcasted_iota(jnp.int32, (16, 128), 1) % 16) == lax.broadcasted_iota(jnp.int32, (16, 128), 0)
    for half in range(2):

        def body(g, carry):
            base = pl.multiple_of(g * 256, 256)
            lo = send[half, :, pl.ds(base, 128)].astype(F32)
            hi = send[half, :, pl.ds(base + 128, 128)].astype(F32)
            for c in range(CH):
                re = jnp.where(mask, jnp.broadcast_to(lo[c : c + 1], (16, 128)), 0.0)
                im = jnp.where(mask, jnp.broadcast_to(hi[c : c + 1], (16, 128)), 0.0)
                r0 = c * 32
                diag[half * 8 + g, r0 : r0 + 16, 0:128] = re.astype(BF16)
                diag[half * 8 + g, r0 : r0 + 16, 128:256] = im.astype(BF16)
                diag[half * 8 + g, r0 + 16 : r0 + 32, 0:128] = im.astype(BF16)
                diag[half * 8 + g, r0 + 16 : r0 + 32, 128:256] = (-re).astype(BF16)
            return carry

        lax.fori_loop(0, 8, body, 0)


def cross_half(whole, diag, cross, row, half):
    def body(g, carry):
        right = whole[half, pl.ds(row, 128), pl.ds(pl.multiple_of(g * 256, 256), 256)]
        gg = half * 8 + g
        k0 = pl.multiple_of(gg * 16, 16)
        res = lax.dot_general(diag[gg], right, (((1,), (1,)), ((), ())), preferred_element_type=F32).astype(BF16)
        for c in range(CH):
            for r in range(2):
                r0 = c * 32 + r * 16
                cross[r, c // 2, pl.ds(k0, 16), (c % 2) * 128 : (c % 2) * 128 + 128] = res[r0 : r0 + 16]
        return carry

    lax.fori_loop(0, 8, body, 0, unroll=8)


def cross_pair(whole, diag, cross, row, row2, half):
    def body(g, carry):
        cols = pl.ds(pl.multiple_of(g * 256, 256), 256)
        right = jnp.concatenate([whole[half, pl.ds(row, 128), cols], whole[half, pl.ds(row2, 128), cols]], axis=0)
        gg = half * 8 + g
        k0 = pl.multiple_of(gg * 16, 16)
        res = lax.dot_general(diag[gg], right, (((1,), (1,)), ((), ())), preferred_element_type=F32).astype(BF16)
        for c in range(CH):
            for r in range(2):
                r0 = c * 32 + r * 16
                cross[r, c, pl.ds(k0, 16), :] = res[r0 : r0 + 16]
        return carry

    lax.fori_loop(0, 8, body, 0, unroll=8)


def both_sides(table, re, im):
    even = jnp.dot(table[0], re, preferred_element_type=F32)
    odd = jnp.dot(table[1], im, preferred_element_type=F32)
    return (even + odd).astype(BF16), (even - odd).astype(BF16)


def lags_of(table, cross, scr):
    def body(cp, carry):
        later, earlier = both_sides(table, cross[0, cp], cross[1, cp])
        for b in range(2):
            scr[0, 2 * cp + b] = later[:, b * 128 : b * 128 + 128]
            scr[1, 2 * cp + b] = earlier[:, b * 128 : b * 128 + 128]
        return carry

    lax.fori_loop(0, 8, body, 0, unroll=4)


def lags_pair(table, cross, scr):
    def body(c, carry):
        later, earlier = both_sides(table, cross[0, c], cross[1, c])
        for b in range(2):
            scr[b, 0, c] = later[:, b * 128 : b * 128 + 128]
            scr[b, 1, c] = earlier[:, b * 128 : b * 128 + 128]
        return carry

    lax.fori_loop(0, CH, body, 0, unroll=4)


def finish(scr, out):
    def body(i, carry):
        d = pl.multiple_of(i * 16, 16)
        out[pl.ds(HALF + d, 16)] = jnp.swapaxes(scr[0, :, pl.ds(d, 16), :], 0, 1)
        earlier = jnp.swapaxes(scr[1, :, pl.ds(d, 16), :], 0, 1)
        for u in range(16):
            out[HALF - d - u] = earlier[u]
        return carry

    lax.fori_loop(0, HALF // 16, body, 0, unroll=2)
    out[0] = jnp.swapaxes(scr[1, :, HALF : HALF + 16, :], 0, 1)[0]


def flip(z_lo, bits):
    if bits & 1:
        z_lo = z_lo + 1 - 2 * lax.rem(z_lo, 2)
    if bits & 2:
        z_lo = lax.rem(z_lo + 2, 4)
    return z_lo


OFFSETS = (0, -1, 1, 2)


def parts_of(half, dx, dy):
    first, second = (dx, dy) if half == 0 else (dy, dx)
    if second == 2 or (second == 0 and first == 2):
        return ("a", "b")
    return ("ab",)


KEYS = {}
for _half in range(2):
    for _dx in OFFSETS:
        for _dy in OFFSETS:
            if (_dx, _dy) != (0, 0):
                for _part in parts_of(_half, _dx, _dy):
                    KEYS[_half, _dx, _dy, _part] = len(KEYS)

def wrap(offset):
    offset %= 4
    return offset - 4 if offset == 3 else offset


def swap_kernel(code, x_ref, own, pair, xs, land, send_sem, recv_sem):
    grp, dev = lax.axis_index("grp"), lax.axis_index("dev")
    z_lo, core, z_hi = grp // 2, lax.rem(grp, 2), lax.rem(dev, 2)
    partner = flip(z_lo, code >> 1) * 2 + (1 - core if code & 1 else core)
    sides = [(partner, dev), (partner, dev + 1 - 2 * z_hi)]
    active = [1] if code == 0 else [0, 1]

    barrier = pltpu.get_barrier_semaphore()
    for side in active:
        pl.semaphore_signal(barrier, inc=1, device_id=sides[side], device_id_type=MESH)
    prepare(x_ref, xs, own)
    pl.semaphore_wait(barrier, len(active))

    copies = []
    for half in range(2):
        for side in active:
            k = half * 2 + side
            copies.append(pltpu.make_async_remote_copy(
                src_ref=own.at[half], dst_ref=land.at[side, half], send_sem=send_sem.at[k], recv_sem=recv_sem.at[k],
                device_id=sides[side], device_id_type=MESH,
            ))
            copies[-1].start()
    same = pl.multiple_of(z_hi * 16, 16)
    far = pl.multiple_of(16 - z_hi * 16, 16)
    if code == 0:
        for half in range(2):
            pair[half, pl.ds(same, 16), :] = own[half]
    for c in copies:
        c.wait()
    for half in range(2):
        for side in active:
            pair[half, pl.ds(same if side == 0 else far, 16), :] = land[side, half]


def gather_kernel(own, pair, table_hbm, tiles, last, table, diag, whole, cross, scr, send_sem, recv_sem, table_sem):
    grp, dev = lax.axis_index("grp"), lax.axis_index("dev")
    y, x, z_hi = dev // 8, lax.rem(dev // 2, 4), lax.rem(dev, 2)

    def at(off_x, off_y):
        return grp, lax.rem(y + off_y + 4, 4) * 8 + lax.rem(x + off_x + 4, 4) * 2 + z_hi

    steps = {("x", 1): at(1, 0), ("x", -1): at(-1, 0), ("y", 1): at(0, 1), ("y", -1): at(0, -1)}
    fetch = pltpu.make_async_copy(table_hbm, table, table_sem)
    fetch.start()
    barrier = pltpu.get_barrier_semaphore()
    for device in steps.values():
        pl.semaphore_signal(barrier, inc=1, device_id=device, device_id_type=MESH)
    for half in range(2):
        whole[half, pl.ds(pl.multiple_of((y * 8 + x * 2) * 16, 32), 32), :] = pair[half]
    pl.semaphore_wait(barrier, 4)

    started = []

    def block(half, dx, dy, part):
        row = (lax.rem(y + dy + 4, 4) * 8 + lax.rem(x + dx + 4, 4) * 2) * 16
        if part == "ab":
            return whole.at[half, pl.ds(pl.multiple_of(row, 32), 32), :]
        return whole.at[half, pl.ds(pl.multiple_of(row + (16 if part == "b" else 0), 16), 16), :]

    def copy(half, dx, dy, part, k, device):
        ref = block(half, dx, dy, part)
        return pltpu.make_async_remote_copy(
            src_ref=ref, dst_ref=ref, send_sem=send_sem.at[k], recv_sem=recv_sem.at[k],
            device_id=device, device_id_type=MESH,
        )

    def push(half, dx, dy, part, axis, way):
        to = (wrap(dx - way), dy) if axis == "x" else (dx, wrap(dy - way))
        c = copy(half, dx, dy, part, KEYS[half, to[0], to[1], part], steps[axis, way])
        c.start()
        started.append(c)

    def arrive(half, dx, dy):
        for part in parts_of(half, dx, dy):
            copy(half, dx, dy, part, KEYS[half, dx, dy, part], steps["x", 1]).wait_recv()

    axes = (("x", "y"), ("y", "x"))

    def swap(half, a, b):
        return (a, b) if half == 0 else (b, a)

    def send_full(half, a, b, which):
        dx, dy = swap(half, a, b)
        for way in (1, -1):
            push(half, dx, dy, "ab", axes[half][which], way)

    def forward(half, a, b, which):
        dx, dy = swap(half, a, b)
        came = (a, b)[which]
        push(half, dx, dy, "a" if came == -1 else "b", axes[half][which], -came)

    def take(half, a, b):
        arrive(half, *swap(half, a, b))

    for half in range(2):
        send_full(half, 0, 0, 0)
        send_full(half, 0, 0, 1)
    build_diag(own, diag)
    for half in range(2):
        for a in (-1, 1):
            take(half, a, 0)
            forward(half, a, 0, 0)
            send_full(half, a, 0, 1)
    for half in range(2):
        for b in (-1, 1):
            take(half, 0, b)
            forward(half, 0, b, 1)
    for half in range(2):
        take(half, 2, 0)
        send_full(half, 2, 0, 1)

    def row_of(dy):
        return pl.multiple_of(lax.rem(y + dy + 4, 4) * 128, 128)

    fetch.wait()
    first = cross.at[:, 0:8]
    cross_half(whole, diag, first, row_of(0), 0)
    for half in range(2):
        for a in (-1, 1):
            for b in (-1, 1):
                take(half, a, b)
                forward(half, a, b, 1)
    arrive(1, 2, 0)
    cross_half(whole, diag, first, row_of(0), 1)
    for half in range(2):
        for b in (-1, 1):
            take(half, 2, b)
            forward(half, 2, b, 1)
    lags_of(table, first, scr.at[0])
    finish(scr.at[0], tiles.at[0])
    cross_pair(whole, diag, cross, row_of(-1), row_of(1), 0)
    arrive(1, 2, -1)
    arrive(1, 2, 1)
    cross_pair(whole, diag, cross, row_of(-1), row_of(1), 1)
    lags_pair(table, cross, scr)
    finish(scr.at[0], tiles.at[1])
    finish(scr.at[1], tiles.at[2])
    for dx in OFFSETS:
        arrive(0, dx, 2)
    cross_half(whole, diag, last, row_of(2), 0)
    arrive(1, 2, 2)
    cross_half(whole, diag, last, row_of(2), 1)
    for c in started:
        c.wait_send()


def write_kernel(tiles, last, table, out, scr, stage, sem):
    y = lax.axis_index("dev") // 8

    def put(src, dy, k):
        lanes = pl.multiple_of(lax.rem(y + dy + 4, 4) * 128, 128)
        part = LAGS // PIECES
        return [
            pltpu.make_async_copy(
                src.at[pl.ds(i * part, part)], out.at[pl.ds(i * part, part), :, pl.ds(lanes, 128)], sem.at[k * PIECES + i]
            )
            for i in range(PIECES)
        ]

    copies = []
    for i, dy in enumerate((0, -1, 1)):
        copies += put(tiles.at[i], dy, i)
    for c in copies:
        c.start()
    lags_of(table, last, scr)
    finish(scr, stage)
    final = put(stage, 2, 3)
    for c in final:
        c.start()
    for c in copies + final:
        c.wait()


def on_device(spectra, round_mask):
    mask = jnp.mod(round_mask[0], lax.axis_size("grp"))
    table = jnp.asarray(make_tables())
    vmem = pl.BlockSpec(memory_space=pltpu.VMEM)

    def swap(code, block):
        return pl.pallas_call(
            functools.partial(swap_kernel, code),
            out_shape=(pltpu.VMEM((2, CH, 2048), BF16), pltpu.VMEM((2, 2 * CH, 2048), BF16)),
            in_specs=[vmem],
            out_specs=(vmem, vmem),
            scratch_shapes=[
                pltpu.VMEM((2, 256, 128), F32),
                pltpu.VMEM((2, 2, CH, 2048), BF16),
                pltpu.SemaphoreType.DMA((4,)),
                pltpu.SemaphoreType.DMA((4,)),
            ],
            compiler_params=pltpu.CompilerParams(
                collective_id=code, has_side_effects=True, vmem_limit_bytes=8 * 2**20
            ),
            name=f"swap_{code}",
        )(block)

    own, pair = lax.switch(mask, [functools.partial(swap, code) for code in range(8)], spectra)
    tiles, last, table = pl.pallas_call(
        gather_kernel,
        out_shape=(
            pltpu.VMEM((3, LAGS, CH, 128), BF16),
            pltpu.VMEM((2, 8, NF, 256), BF16),
            pltpu.VMEM((2, ROWS, NF), BF16),
        ),
        in_specs=[vmem, vmem, pl.BlockSpec(memory_space=pltpu.HBM)],
        out_specs=(vmem, vmem, vmem),
        scratch_shapes=[
            pltpu.VMEM((16, 512, 256), BF16),
            pltpu.VMEM((2, 512, 2048), BF16),
            pltpu.VMEM((2, CH, NF, 256), BF16),
            pltpu.VMEM((2, 2, CH, ROWS, 128), BF16),
            pltpu.SemaphoreType.DMA((len(KEYS),)),
            pltpu.SemaphoreType.DMA((len(KEYS),)),
            pltpu.SemaphoreType.DMA,
        ],
        compiler_params=pltpu.CompilerParams(collective_id=8, has_side_effects=True, vmem_limit_bytes=24 * 2**20),
        name="gather",
    )(own, pair, pltpu.with_memory_space_constraint(table, pltpu.HBM))
    return pl.pallas_call(
        write_kernel,
        out_shape=jax.ShapeDtypeStruct((LAGS, CH, 512), BF16),
        in_specs=[vmem] * 3,
        out_specs=pl.BlockSpec(memory_space=pl.ANY),
        scratch_shapes=[
            pltpu.VMEM((2, CH, ROWS, 128), BF16),
            pltpu.VMEM((LAGS, CH, 128), BF16),
            pltpu.SemaphoreType.DMA((4 * PIECES,)),
        ],
        compiler_params=pltpu.CompilerParams(vmem_limit_bytes=24 * 2**20),
        name="write",
    )(tiles, last, table)


def solution(mesh):
    return jax.shard_map(
        on_device,
        mesh=mesh,
        in_specs=(P(("grp", "dev"), None, None), P()),
        out_specs=P(None, ("grp", "dev"), None),
        check_vma=False,
    )
```

```python
import functools
import math

import jax
import jax.numpy as jnp
import numpy as np
from jax import lax
from jax.experimental import pallas as pl
from jax.experimental.pallas import tpu as pltpu
from jax.sharding import PartitionSpec as P

MESH = pl.DeviceIdType.MESH
NF = 256
WINDOWS = 8
LAGS = 768
HALF = LAGS // 2
FREQ_LO = 64
NFFT = 1024
ROWS = 400
CH = 16
PIECES = 4
F32, BF16 = jnp.float32, jnp.bfloat16


def make_tables():
    freq = np.arange(NF)
    steps = ((FREQ_LO + freq)[None, :] * np.arange(ROWS)[:, None]) % NFFT
    theta = 2.0 * math.pi / NFFT * steps
    taper = (0.5 - 0.5 * np.cos(2.0 * math.pi * (freq + 0.5) / NF)) / math.sqrt(2.0 * WINDOWS * NF)
    return np.stack([taper * np.cos(theta), -taper * np.sin(theta)]).astype(jnp.bfloat16)


def prepare(x_ref, xs, send):
    for half in range(2):
        xs[half] = x_ref[:, :, half * 128 : half * 128 + 128].reshape(256, 128).astype(F32)
    lane = lax.broadcasted_iota(jnp.int32, (CH, 128), 1) // 16
    for half in range(2):
        for h in range(2):
            rows = [xs[half, pl.ds(8 * h + w, CH, stride=16), :] for w in range(8)]
            for g in range(8):
                acc = None
                for w in range(8):
                    shift = ((w - g) * 16) % 128
                    v = rows[w] if shift == 0 else pltpu.roll(rows[w], shift, 1)
                    acc = v if acc is None else jnp.where(lane == w, v, acc)
                first = g * 256 + h * 128
                send[half, :, first : first + 128] = acc.astype(BF16)


def build_diag(send, diag):
    mask = (lax.broadcasted_iota(jnp.int32, (16, 128), 1) % 16) == lax.broadcasted_iota(jnp.int32, (16, 128), 0)
    for half in range(2):

        def body(g, carry):
            base = pl.multiple_of(g * 256, 256)
            lo = send[half, :, pl.ds(base, 128)].astype(F32)
            hi = send[half, :, pl.ds(base + 128, 128)].astype(F32)
            for c in range(CH):
                re = jnp.where(mask, jnp.broadcast_to(lo[c : c + 1], (16, 128)), 0.0)
                im = jnp.where(mask, jnp.broadcast_to(hi[c : c + 1], (16, 128)), 0.0)
                r0 = c * 32
                diag[half * 8 + g, r0 : r0 + 16, 0:128] = re.astype(BF16)
                diag[half * 8 + g, r0 : r0 + 16, 128:256] = im.astype(BF16)
                diag[half * 8 + g, r0 + 16 : r0 + 32, 0:128] = im.astype(BF16)
                diag[half * 8 + g, r0 + 16 : r0 + 32, 128:256] = (-re).astype(BF16)
            return carry

        lax.fori_loop(0, 8, body, 0)


def cross_half(whole, diag, cross, row, half, beside=None):
    def body(g, carry):
        right = whole[half, pl.ds(row, 128), pl.ds(pl.multiple_of(g * 256, 256), 256)]
        gg = half * 8 + g
        k0 = pl.multiple_of(gg * 16, 16)
        res = lax.dot_general(diag[gg], right, (((1,), (1,)), ((), ())), preferred_element_type=F32).astype(BF16)
        for c in range(CH):
            for r in range(2):
                r0 = c * 32 + r * 16
                cross[r, c // 2, pl.ds(k0, 16), (c % 2) * 128 : (c % 2) * 128 + 128] = res[r0 : r0 + 16]
        if beside is not None:
            beside(g)
        return carry

    lax.fori_loop(0, 8, body, 0, unroll=8)


def cross_pair(whole, diag, cross, row, row2, half, beside=None):
    def body(g, carry):
        cols = pl.ds(pl.multiple_of(g * 256, 256), 256)
        right = jnp.concatenate([whole[half, pl.ds(row, 128), cols], whole[half, pl.ds(row2, 128), cols]], axis=0)
        gg = half * 8 + g
        k0 = pl.multiple_of(gg * 16, 16)
        res = lax.dot_general(diag[gg], right, (((1,), (1,)), ((), ())), preferred_element_type=F32).astype(BF16)
        for c in range(CH):
            for r in range(2):
                r0 = c * 32 + r * 16
                cross[r, c, pl.ds(k0, 16), :] = res[r0 : r0 + 16]
        if beside is not None:
            beside(g)
        return carry

    lax.fori_loop(0, 8, body, 0, unroll=8)


def both_sides(table, re, im):
    even = jnp.dot(table[0], re, preferred_element_type=F32)
    odd = jnp.dot(table[1], im, preferred_element_type=F32)
    return (even + odd).astype(BF16), (even - odd).astype(BF16)


def lags_of(table, cross, scr):
    def body(cp, carry):
        later, earlier = both_sides(table, cross[0, cp], cross[1, cp])
        for b in range(2):
            scr[0, 2 * cp + b] = later[:, b * 128 : b * 128 + 128]
            scr[1, 2 * cp + b] = earlier[:, b * 128 : b * 128 + 128]
        return carry

    lax.fori_loop(0, 8, body, 0, unroll=4)


def lags_pair(table, cross, scr):
    def body(c, carry):
        later, earlier = both_sides(table, cross[0, c], cross[1, c])
        for b in range(2):
            scr[b, 0, c] = later[:, b * 128 : b * 128 + 128]
            scr[b, 1, c] = earlier[:, b * 128 : b * 128 + 128]
        return carry

    lax.fori_loop(0, CH, body, 0, unroll=4)


def finish_step(scr, out, i):
    d = pl.multiple_of(i * 16, 16)
    out[pl.ds(HALF + d, 16)] = jnp.swapaxes(scr[0, :, pl.ds(d, 16), :], 0, 1)
    earlier = jnp.swapaxes(scr[1, :, pl.ds(d, 16), :], 0, 1)
    for u in range(16):
        out[HALF - d - u] = earlier[u]


def finish_end(scr, out):
    out[0] = jnp.swapaxes(scr[1, :, HALF : HALF + 16, :], 0, 1)[0]


def finish_beside(scr, out):
    def beside(g):
        for u in range(3):
            finish_step(scr, out, g * 3 + u)

    return beside


def flip(z_lo, bits):
    if bits & 1:
        z_lo = z_lo + 1 - 2 * lax.rem(z_lo, 2)
    if bits & 2:
        z_lo = lax.rem(z_lo + 2, 4)
    return z_lo


OFFSETS = (0, -1, 1, 2)


def parts_of(half, dx, dy):
    first, second = (dx, dy) if half == 0 else (dy, dx)
    if second == 2 or (second == 0 and first == 2):
        return ("a", "b")
    return ("ab",)


KEYS = {}
for _half in range(2):
    for _dx in OFFSETS:
        for _dy in OFFSETS:
            if (_dx, _dy) != (0, 0):
                for _part in parts_of(_half, _dx, _dy):
                    KEYS[_half, _dx, _dy, _part] = len(KEYS)

def wrap(offset):
    offset %= 4
    return offset - 4 if offset == 3 else offset


def swap_kernel(code, x_ref, own, pair, xs, land, send_sem, recv_sem):
    grp, dev = lax.axis_index("grp"), lax.axis_index("dev")
    z_lo, core, z_hi = grp // 2, lax.rem(grp, 2), lax.rem(dev, 2)
    partner = flip(z_lo, code >> 1) * 2 + (1 - core if code & 1 else core)
    sides = [(partner, dev), (partner, dev + 1 - 2 * z_hi)]
    active = [1] if code == 0 else [0, 1]

    barrier = pltpu.get_barrier_semaphore()
    for side in active:
        pl.semaphore_signal(barrier, inc=1, device_id=sides[side], device_id_type=MESH)
    prepare(x_ref, xs, own)
    pl.semaphore_wait(barrier, len(active))

    copies = []
    for half in range(2):
        for side in active:
            k = half * 2 + side
            copies.append(pltpu.make_async_remote_copy(
                src_ref=own.at[half], dst_ref=land.at[side, half], send_sem=send_sem.at[k], recv_sem=recv_sem.at[k],
                device_id=sides[side], device_id_type=MESH,
            ))
            copies[-1].start()
    same = pl.multiple_of(z_hi * 16, 16)
    far = pl.multiple_of(16 - z_hi * 16, 16)
    if code == 0:
        for half in range(2):
            pair[half, pl.ds(same, 16), :] = own[half]
    for c in copies:
        c.wait()
    for half in range(2):
        for side in active:
            pair[half, pl.ds(same if side == 0 else far, 16), :] = land[side, half]


def gather_kernel(
    own, pair, table_hbm, tile, scr, diag, far, table, whole, cross, scr0, send_sem, recv_sem, table_sem
):
    grp, dev = lax.axis_index("grp"), lax.axis_index("dev")
    y, x, z_hi = dev // 8, lax.rem(dev // 2, 4), lax.rem(dev, 2)

    def at(off_x, off_y):
        return grp, lax.rem(y + off_y + 4, 4) * 8 + lax.rem(x + off_x + 4, 4) * 2 + z_hi

    steps = {("x", 1): at(1, 0), ("x", -1): at(-1, 0), ("y", 1): at(0, 1), ("y", -1): at(0, -1)}
    fetch = pltpu.make_async_copy(table_hbm, table, table_sem)
    fetch.start()
    barrier = pltpu.get_barrier_semaphore()
    for device in steps.values():
        pl.semaphore_signal(barrier, inc=1, device_id=device, device_id_type=MESH)
    for half in range(2):
        whole[half, pl.ds(pl.multiple_of((y * 8 + x * 2) * 16, 32), 32), :] = pair[half]
    pl.semaphore_wait(barrier, 4)

    started = []

    def block(half, dx, dy, part):
        row = (lax.rem(y + dy + 4, 4) * 8 + lax.rem(x + dx + 4, 4) * 2) * 16
        if part == "ab":
            return whole.at[half, pl.ds(pl.multiple_of(row, 32), 32), :]
        return whole.at[half, pl.ds(pl.multiple_of(row + (16 if part == "b" else 0), 16), 16), :]

    def copy(half, dx, dy, part, k, device):
        ref = block(half, dx, dy, part)
        return pltpu.make_async_remote_copy(
            src_ref=ref, dst_ref=ref, send_sem=send_sem.at[k], recv_sem=recv_sem.at[k],
            device_id=device, device_id_type=MESH,
        )

    def push(half, dx, dy, part, axis, way):
        to = (wrap(dx - way), dy) if axis == "x" else (dx, wrap(dy - way))
        c = copy(half, dx, dy, part, KEYS[half, to[0], to[1], part], steps[axis, way])
        c.start()
        started.append(c)

    def arrive(half, dx, dy):
        for part in parts_of(half, dx, dy):
            copy(half, dx, dy, part, KEYS[half, dx, dy, part], steps["x", 1]).wait_recv()

    axes = (("x", "y"), ("y", "x"))

    def swap(half, a, b):
        return (a, b) if half == 0 else (b, a)

    def send_full(half, a, b, which):
        dx, dy = swap(half, a, b)
        for way in (1, -1):
            push(half, dx, dy, "ab", axes[half][which], way)

    def forward(half, a, b, which):
        dx, dy = swap(half, a, b)
        came = (a, b)[which]
        push(half, dx, dy, "a" if came == -1 else "b", axes[half][which], -came)

    def take(half, a, b):
        arrive(half, *swap(half, a, b))

    for half in range(2):
        send_full(half, 0, 0, 0)
    build_diag(own, diag)
    for half in range(2):
        send_full(half, 0, 0, 1)
    for half in range(2):
        for a in (-1, 1):
            take(half, a, 0)
            forward(half, a, 0, 0)
            send_full(half, a, 0, 1)
    for b in (-1, 1):
        take(1, 0, b)
        forward(1, 0, b, 1)
    take(0, 2, 0)
    send_full(0, 2, 0, 1)

    def row_of(dy):
        return pl.multiple_of(lax.rem(y + dy + 4, 4) * 128, 128)

    fetch.wait()
    first = cross.at[:, 0:8]
    cross_half(whole, diag, first, row_of(0), 0)
    for a in (-1, 1):
        for b in (-1, 1):
            take(1, a, b)
            forward(1, a, b, 1)
    for b in (-1, 1):
        take(0, 0, b)
        forward(0, 0, b, 1)
    take(1, 2, 0)
    send_full(1, 2, 0, 1)
    arrive(1, 2, 0)
    cross_half(whole, diag, first, row_of(0), 1)
    for a in (-1, 1):
        for b in (-1, 1):
            take(0, a, b)
            forward(0, a, b, 1)
    lags_of(table, first, scr0)
    for b in (-1, 1):
        take(0, 2, b)
        forward(0, 2, b, 1)
    cross_pair(whole, diag, cross, row_of(-1), row_of(1), 0, finish_beside(scr0, tile))
    finish_end(scr0, tile)
    for b in (-1, 1):
        take(1, 2, b)
        forward(1, 2, b, 1)
    arrive(1, 2, -1)
    arrive(1, 2, 1)
    cross_pair(whole, diag, cross, row_of(-1), row_of(1), 1)
    lags_pair(table, cross, scr)
    for dx in OFFSETS:
        arrive(0, dx, 2)
    arrive(1, 2, 2)
    for half in range(2):
        far[half] = whole[half, pl.ds(row_of(2), 128), :]
    for c in started:
        c.wait_send()


def write_kernel(tile, scr, diag, far, table, out, cross, scr0, stage, sem):
    y = lax.axis_index("dev") // 8

    def put(src, dy, k):
        lanes = pl.multiple_of(lax.rem(y + dy + 4, 4) * 128, 128)
        part = LAGS // PIECES
        return [
            pltpu.make_async_copy(
                src.at[pl.ds(i * part, part)], out.at[pl.ds(i * part, part), :, pl.ds(lanes, 128)], sem.at[k * PIECES + i]
            )
            for i in range(PIECES)
        ]

    copies = []

    def write(src, dy):
        mine = put(src, dy, len(copies) // PIECES)
        for c in mine:
            c.start()
        copies.extend(mine)

    write(tile, 0)
    for half, dy in enumerate((-1, 1)):
        cross_half(far, diag, cross, 0, half, finish_beside(scr.at[half], stage.at[half]))
        finish_end(scr.at[half], stage.at[half])
        write(stage.at[half], dy)
    lags_of(table, cross, scr0)
    lanes = pl.multiple_of(lax.rem(y + 2, 4) * 128, 128)
    quarter = HALF // 4

    def send_rows(first, count):
        k = len(copies)
        c = pltpu.make_async_copy(
            stage.at[2, pl.ds(first, count)], out.at[pl.ds(first, count), :, pl.ds(lanes, 128)], sem.at[k]
        )
        c.start()
        copies.append(c)

    for q in range(4):

        def body(i, carry, q=q):
            finish_step(scr0, stage.at[2], q * (quarter // 16) + i)
            return carry

        lax.fori_loop(0, quarter // 16, body, 0, unroll=2)
        if q == 3:
            finish_end(scr0, stage.at[2])
        send_rows(HALF + q * quarter, quarter)
        low = HALF - (q + 1) * quarter + 1 if q < 3 else 0
        send_rows(low, (HALF - q * quarter if q else HALF - 1) - low + 1)
    for c in copies:
        c.wait()


def on_device(spectra, round_mask):
    mask = jnp.mod(round_mask[0], lax.axis_size("grp"))
    table = jnp.asarray(make_tables())
    vmem = pl.BlockSpec(memory_space=pltpu.VMEM)

    def swap(code, block):
        return pl.pallas_call(
            functools.partial(swap_kernel, code),
            out_shape=(pltpu.VMEM((2, CH, 2048), BF16), pltpu.VMEM((2, 2 * CH, 2048), BF16)),
            in_specs=[vmem],
            out_specs=(vmem, vmem),
            scratch_shapes=[
                pltpu.VMEM((2, 256, 128), F32),
                pltpu.VMEM((2, 2, CH, 2048), BF16),
                pltpu.SemaphoreType.DMA((4,)),
                pltpu.SemaphoreType.DMA((4,)),
            ],
            compiler_params=pltpu.CompilerParams(
                collective_id=code, has_side_effects=True, vmem_limit_bytes=8 * 2**20
            ),
            name=f"swap_{code}",
        )(block)

    own, pair = lax.switch(mask, [functools.partial(swap, code) for code in range(8)], spectra)
    parts = pl.pallas_call(
        gather_kernel,
        out_shape=(
            pltpu.VMEM((LAGS, CH, 128), BF16),
            pltpu.VMEM((2, 2, CH, ROWS, 128), BF16),
            pltpu.VMEM((16, 512, 256), BF16),
            pltpu.VMEM((2, 128, 2048), BF16),
            pltpu.VMEM((2, ROWS, NF), BF16),
        ),
        in_specs=[vmem, vmem, pl.BlockSpec(memory_space=pltpu.HBM)],
        out_specs=(vmem,) * 5,
        scratch_shapes=[
            pltpu.VMEM((2, 512, 2048), BF16),
            pltpu.VMEM((2, CH, NF, 256), BF16),
            pltpu.VMEM((2, CH, ROWS, 128), BF16),
            pltpu.SemaphoreType.DMA((len(KEYS),)),
            pltpu.SemaphoreType.DMA((len(KEYS),)),
            pltpu.SemaphoreType.DMA,
        ],
        compiler_params=pltpu.CompilerParams(collective_id=8, has_side_effects=True, vmem_limit_bytes=16 * 2**20),
        name="gather",
    )(own, pair, pltpu.with_memory_space_constraint(table, pltpu.HBM))
    return pl.pallas_call(
        write_kernel,
        out_shape=jax.ShapeDtypeStruct((LAGS, CH, 512), BF16),
        in_specs=[vmem] * 5,
        out_specs=pl.BlockSpec(memory_space=pl.ANY),
        scratch_shapes=[
            pltpu.VMEM((2, 8, NF, 256), BF16),
            pltpu.VMEM((2, CH, ROWS, 128), BF16),
            pltpu.VMEM((3, LAGS, CH, 128), BF16),
            pltpu.SemaphoreType.DMA((3 * PIECES + 8,)),
        ],
        compiler_params=pltpu.CompilerParams(vmem_limit_bytes=20 * 2**20),
        name="write",
    )(*parts)


def solution(mesh):
    return jax.shard_map(
        on_device,
        mesh=mesh,
        in_specs=(P(("grp", "dev"), None, None), P()),
        out_specs=P(None, ("grp", "dev"), None),
        check_vma=False,
    )
```

```python
import functools
import math

import jax
import jax.numpy as jnp
import numpy as np
from jax import lax
from jax.experimental import pallas as pl
from jax.experimental.pallas import tpu as pltpu
from jax.sharding import PartitionSpec as P

MESH = pl.DeviceIdType.MESH
NF = 256
WINDOWS = 8
LAGS = 768
HALF = LAGS // 2
FREQ_LO = 64
NFFT = 1024
ROWS = 400
CH = 16
PIECES = 4
F32, BF16 = jnp.float32, jnp.bfloat16


def make_tables():
    freq = np.arange(NF)
    steps = ((FREQ_LO + freq)[None, :] * np.arange(ROWS)[:, None]) % NFFT
    theta = 2.0 * math.pi / NFFT * steps
    taper = (0.5 - 0.5 * np.cos(2.0 * math.pi * (freq + 0.5) / NF)) / math.sqrt(2.0 * WINDOWS * NF)
    return np.stack([taper * np.cos(theta), -taper * np.sin(theta)]).astype(jnp.bfloat16)


def prepare(x_ref, xs, send):
    for half in range(2):
        xs[half] = x_ref[:, :, half * 128 : half * 128 + 128].reshape(256, 128).astype(F32)
    lane = lax.broadcasted_iota(jnp.int32, (CH, 128), 1) // 16
    for half in range(2):
        for h in range(2):
            rows = [xs[half, pl.ds(8 * h + w, CH, stride=16), :] for w in range(8)]
            for g in range(8):
                acc = None
                for w in range(8):
                    shift = ((w - g) * 16) % 128
                    v = rows[w] if shift == 0 else pltpu.roll(rows[w], shift, 1)
                    acc = v if acc is None else jnp.where(lane == w, v, acc)
                first = g * 256 + h * 128
                send[half, :, first : first + 128] = acc.astype(BF16)


def build_diag(send, diag):
    mask = (lax.broadcasted_iota(jnp.int32, (16, 128), 1) % 16) == lax.broadcasted_iota(jnp.int32, (16, 128), 0)
    for half in range(2):

        def body(g, carry):
            base = pl.multiple_of(g * 256, 256)
            lo = send[half, :, pl.ds(base, 128)].astype(F32)
            hi = send[half, :, pl.ds(base + 128, 128)].astype(F32)
            for c in range(CH):
                re = jnp.where(mask, jnp.broadcast_to(lo[c : c + 1], (16, 128)), 0.0)
                im = jnp.where(mask, jnp.broadcast_to(hi[c : c + 1], (16, 128)), 0.0)
                r0 = c * 32
                diag[half * 8 + g, r0 : r0 + 16, 0:128] = re.astype(BF16)
                diag[half * 8 + g, r0 : r0 + 16, 128:256] = im.astype(BF16)
                diag[half * 8 + g, r0 + 16 : r0 + 32, 0:128] = im.astype(BF16)
                diag[half * 8 + g, r0 + 16 : r0 + 32, 128:256] = (-re).astype(BF16)
            return carry

        lax.fori_loop(0, 8, body, 0)


def cross_half(whole, diag, cross, row, half, beside=None):
    def body(g, carry):
        right = whole[half, pl.ds(row, 128), pl.ds(pl.multiple_of(g * 256, 256), 256)]
        gg = half * 8 + g
        k0 = pl.multiple_of(gg * 16, 16)
        res = lax.dot_general(diag[gg], right, (((1,), (1,)), ((), ())), preferred_element_type=F32).astype(BF16)
        for c in range(CH):
            for r in range(2):
                r0 = c * 32 + r * 16
                cross[r, c // 2, pl.ds(k0, 16), (c % 2) * 128 : (c % 2) * 128 + 128] = res[r0 : r0 + 16]
        if beside is not None:
            beside(g)
        return carry

    lax.fori_loop(0, 8, body, 0, unroll=8)


def cross_pair(whole, diag, cross, row, row2, half, beside=None):
    def body(g, carry):
        cols = pl.ds(pl.multiple_of(g * 256, 256), 256)
        right = jnp.concatenate([whole[half, pl.ds(row, 128), cols], whole[half, pl.ds(row2, 128), cols]], axis=0)
        gg = half * 8 + g
        k0 = pl.multiple_of(gg * 16, 16)
        res = lax.dot_general(diag[gg], right, (((1,), (1,)), ((), ())), preferred_element_type=F32).astype(BF16)
        for c in range(CH):
            for r in range(2):
                r0 = c * 32 + r * 16
                cross[r, c, pl.ds(k0, 16), :] = res[r0 : r0 + 16]
        if beside is not None:
            beside(g)
        return carry

    lax.fori_loop(0, 8, body, 0, unroll=8)


def both_sides(table, re, im):
    even = jnp.dot(table[0], re, preferred_element_type=F32)
    odd = jnp.dot(table[1], im, preferred_element_type=F32)
    return (even + odd).astype(BF16), (even - odd).astype(BF16)


def lags_of(table, cross, scr):
    def body(cp, carry):
        later, earlier = both_sides(table, cross[0, cp], cross[1, cp])
        for b in range(2):
            scr[0, 2 * cp + b] = later[:, b * 128 : b * 128 + 128]
            scr[1, 2 * cp + b] = earlier[:, b * 128 : b * 128 + 128]
        return carry

    lax.fori_loop(0, 8, body, 0, unroll=4)


def lags_pair(table, cross, scr):
    def body(c, carry):
        later, earlier = both_sides(table, cross[0, c], cross[1, c])
        for b in range(2):
            scr[b, 0, c] = later[:, b * 128 : b * 128 + 128]
            scr[b, 1, c] = earlier[:, b * 128 : b * 128 + 128]
        return carry

    lax.fori_loop(0, CH, body, 0, unroll=4)


def finish_step(scr, out, i):
    d = pl.multiple_of(i * 16, 16)
    out[pl.ds(HALF + d, 16)] = jnp.swapaxes(scr[0, :, pl.ds(d, 16), :], 0, 1)
    earlier = jnp.swapaxes(scr[1, :, pl.ds(d, 16), :], 0, 1)
    for u in range(16):
        out[HALF - d - u] = earlier[u]


def finish_end(scr, out):
    out[0] = jnp.swapaxes(scr[1, :, HALF : HALF + 16, :], 0, 1)[0]


def finish_beside(scr, out):
    def beside(g):
        for u in range(3):
            finish_step(scr, out, g * 3 + u)

    return beside


def flip(z_lo, bits):
    if bits & 1:
        z_lo = z_lo + 1 - 2 * lax.rem(z_lo, 2)
    if bits & 2:
        z_lo = lax.rem(z_lo + 2, 4)
    return z_lo


OFFSETS = (0, -1, 1, 2)


def parts_of(half, dx, dy):
    first, second = (dx, dy) if half == 0 else (dy, dx)
    if second == 2 or (second == 0 and first == 2):
        return ("a", "b")
    return ("ab",)


KEYS = {}
for _half in range(2):
    for _dx in OFFSETS:
        for _dy in OFFSETS:
            if (_dx, _dy) != (0, 0):
                for _part in parts_of(_half, _dx, _dy):
                    KEYS[_half, _dx, _dy, _part] = len(KEYS)

def wrap(offset):
    offset %= 4
    return offset - 4 if offset == 3 else offset


def swap_kernel(code, x_ref, own, pair, xs, land, send_sem, recv_sem):
    grp, dev = lax.axis_index("grp"), lax.axis_index("dev")
    z_lo, core, z_hi = grp // 2, lax.rem(grp, 2), lax.rem(dev, 2)
    partner = flip(z_lo, code >> 1) * 2 + (1 - core if code & 1 else core)
    sides = [(partner, dev), (partner, dev + 1 - 2 * z_hi)]
    active = [1] if code == 0 else [0, 1]

    barrier = pltpu.get_barrier_semaphore()
    for side in active:
        pl.semaphore_signal(barrier, inc=1, device_id=sides[side], device_id_type=MESH)
    prepare(x_ref, xs, own)
    pl.semaphore_wait(barrier, len(active))

    copies = []
    for half in range(2):
        for side in active:
            k = half * 2 + side
            copies.append(pltpu.make_async_remote_copy(
                src_ref=own.at[half], dst_ref=land.at[side, half], send_sem=send_sem.at[k], recv_sem=recv_sem.at[k],
                device_id=sides[side], device_id_type=MESH,
            ))
            copies[-1].start()
    same = pl.multiple_of(z_hi * 16, 16)
    far = pl.multiple_of(16 - z_hi * 16, 16)
    if code == 0:
        for half in range(2):
            pair[half, pl.ds(same, 16), :] = own[half]
    for c in copies:
        c.wait()
    for half in range(2):
        for side in active:
            pair[half, pl.ds(same if side == 0 else far, 16), :] = land[side, half]


def gather_kernel(
    own, pair, table_hbm, tile, scr, diag, far, table, whole, cross, scr0, send_sem, recv_sem, table_sem
):
    grp, dev = lax.axis_index("grp"), lax.axis_index("dev")
    y, x, z_hi = dev // 8, lax.rem(dev // 2, 4), lax.rem(dev, 2)

    def at(off_x, off_y):
        return grp, lax.rem(y + off_y + 4, 4) * 8 + lax.rem(x + off_x + 4, 4) * 2 + z_hi

    steps = {("x", 1): at(1, 0), ("x", -1): at(-1, 0), ("y", 1): at(0, 1), ("y", -1): at(0, -1)}
    fetch = pltpu.make_async_copy(table_hbm, table, table_sem)
    fetch.start()
    barrier = pltpu.get_barrier_semaphore()
    for device in steps.values():
        pl.semaphore_signal(barrier, inc=1, device_id=device, device_id_type=MESH)
    for half in range(2):
        whole[half, pl.ds(pl.multiple_of((y * 8 + x * 2) * 16, 32), 32), :] = pair[half]
    build_diag(own, diag)
    pl.semaphore_wait(barrier, 4)

    started = []

    def block(half, dx, dy, part):
        row = (lax.rem(y + dy + 4, 4) * 8 + lax.rem(x + dx + 4, 4) * 2) * 16
        if part == "ab":
            return whole.at[half, pl.ds(pl.multiple_of(row, 32), 32), :]
        return whole.at[half, pl.ds(pl.multiple_of(row + (16 if part == "b" else 0), 16), 16), :]

    def copy(half, dx, dy, part, k, device):
        ref = block(half, dx, dy, part)
        return pltpu.make_async_remote_copy(
            src_ref=ref, dst_ref=ref, send_sem=send_sem.at[k], recv_sem=recv_sem.at[k],
            device_id=device, device_id_type=MESH,
        )

    def push(half, dx, dy, part, axis, way):
        to = (wrap(dx - way), dy) if axis == "x" else (dx, wrap(dy - way))
        c = copy(half, dx, dy, part, KEYS[half, to[0], to[1], part], steps[axis, way])
        c.start()
        started.append(c)

    def arrive(half, dx, dy):
        for part in parts_of(half, dx, dy):
            copy(half, dx, dy, part, KEYS[half, dx, dy, part], steps["x", 1]).wait_recv()

    axes = (("x", "y"), ("y", "x"))

    def swap(half, a, b):
        return (a, b) if half == 0 else (b, a)

    def send_full(half, a, b, which):
        dx, dy = swap(half, a, b)
        for way in (1, -1):
            push(half, dx, dy, "ab", axes[half][which], way)

    def forward(half, a, b, which):
        dx, dy = swap(half, a, b)
        came = (a, b)[which]
        push(half, dx, dy, "a" if came == -1 else "b", axes[half][which], -came)

    def take(half, a, b):
        arrive(half, *swap(half, a, b))

    for half in range(2):
        send_full(half, 0, 0, 0)
    for half in range(2):
        send_full(half, 0, 0, 1)
    for half in range(2):
        for a in (-1, 1):
            take(half, a, 0)
            forward(half, a, 0, 0)
            send_full(half, a, 0, 1)
    for b in (-1, 1):
        take(1, 0, b)
        forward(1, 0, b, 1)
    take(0, 2, 0)
    send_full(0, 2, 0, 1)

    def row_of(dy):
        return pl.multiple_of(lax.rem(y + dy + 4, 4) * 128, 128)

    fetch.wait()
    first = cross.at[:, 0:8]
    cross_half(whole, diag, first, row_of(0), 0)
    for b in (-1, 1):
        take(0, 0, b)
        forward(0, 0, b, 1)
    take(1, 2, 0)
    send_full(1, 2, 0, 1)
    for a in (-1, 1):
        for b in (-1, 1):
            take(1, a, b)
            forward(1, a, b, 1)
    arrive(1, 2, 0)
    cross_half(whole, diag, first, row_of(0), 1)
    for a in (-1, 1):
        for b in (-1, 1):
            take(0, a, b)
            forward(0, a, b, 1)
    lags_of(table, first, scr0)
    for b in (-1, 1):
        take(0, 2, b)
        forward(0, 2, b, 1)
    cross_pair(whole, diag, cross, row_of(-1), row_of(1), 0, finish_beside(scr0, tile))
    finish_end(scr0, tile)
    for b in (-1, 1):
        take(1, 2, b)
        forward(1, 2, b, 1)
    arrive(1, 2, -1)
    arrive(1, 2, 1)
    cross_pair(whole, diag, cross, row_of(-1), row_of(1), 1)
    lags_pair(table, cross, scr)
    for dx in OFFSETS:
        arrive(0, dx, 2)
    arrive(1, 2, 2)
    for half in range(2):
        far[half] = whole[half, pl.ds(row_of(2), 128), :]
    for c in started:
        c.wait_send()


def write_kernel(tile, scr, diag, far, table, out, cross, scr0, stage, sem):
    y = lax.axis_index("dev") // 8

    def put(src, dy, k):
        lanes = pl.multiple_of(lax.rem(y + dy + 4, 4) * 128, 128)
        part = LAGS // PIECES
        return [
            pltpu.make_async_copy(
                src.at[pl.ds(i * part, part)], out.at[pl.ds(i * part, part), :, pl.ds(lanes, 128)], sem.at[k * PIECES + i]
            )
            for i in range(PIECES)
        ]

    copies = []

    def write(src, dy):
        mine = put(src, dy, len(copies) // PIECES)
        for c in mine:
            c.start()
        copies.extend(mine)

    write(tile, 0)
    for half, dy in enumerate((-1, 1)):
        cross_half(far, diag, cross, 0, half, finish_beside(scr.at[half], stage.at[half]))
        finish_end(scr.at[half], stage.at[half])
        write(stage.at[half], dy)
    lags_of(table, cross, scr0)
    lanes = pl.multiple_of(lax.rem(y + 2, 4) * 128, 128)
    quarter = HALF // 4

    def send_rows(first, count):
        k = len(copies)
        c = pltpu.make_async_copy(
            stage.at[2, pl.ds(first, count)], out.at[pl.ds(first, count), :, pl.ds(lanes, 128)], sem.at[k]
        )
        c.start()
        copies.append(c)

    for q in range(4):

        def body(i, carry, q=q):
            finish_step(scr0, stage.at[2], q * (quarter // 16) + i)
            return carry

        lax.fori_loop(0, quarter // 16, body, 0, unroll=2)
        if q == 3:
            finish_end(scr0, stage.at[2])
        send_rows(HALF + q * quarter, quarter)
        low = HALF - (q + 1) * quarter + 1 if q < 3 else 0
        send_rows(low, (HALF - q * quarter if q else HALF - 1) - low + 1)
    for c in copies:
        c.wait()


def on_device(spectra, round_mask):
    mask = jnp.mod(round_mask[0], lax.axis_size("grp"))
    table = jnp.asarray(make_tables())
    vmem = pl.BlockSpec(memory_space=pltpu.VMEM)

    def swap(code, block):
        return pl.pallas_call(
            functools.partial(swap_kernel, code),
            out_shape=(pltpu.VMEM((2, CH, 2048), BF16), pltpu.VMEM((2, 2 * CH, 2048), BF16)),
            in_specs=[vmem],
            out_specs=(vmem, vmem),
            scratch_shapes=[
                pltpu.VMEM((2, 256, 128), F32),
                pltpu.VMEM((2, 2, CH, 2048), BF16),
                pltpu.SemaphoreType.DMA((4,)),
                pltpu.SemaphoreType.DMA((4,)),
            ],
            compiler_params=pltpu.CompilerParams(
                collective_id=code, has_side_effects=True, vmem_limit_bytes=8 * 2**20
            ),
            name=f"swap_{code}",
        )(block)

    own, pair = lax.switch(mask, [functools.partial(swap, code) for code in range(8)], spectra)
    parts = pl.pallas_call(
        gather_kernel,
        out_shape=(
            pltpu.VMEM((LAGS, CH, 128), BF16),
            pltpu.VMEM((2, 2, CH, ROWS, 128), BF16),
            pltpu.VMEM((16, 512, 256), BF16),
            pltpu.VMEM((2, 128, 2048), BF16),
            pltpu.VMEM((2, ROWS, NF), BF16),
        ),
        in_specs=[vmem, vmem, pl.BlockSpec(memory_space=pltpu.HBM)],
        out_specs=(vmem,) * 5,
        scratch_shapes=[
            pltpu.VMEM((2, 512, 2048), BF16),
            pltpu.VMEM((2, CH, NF, 256), BF16),
            pltpu.VMEM((2, CH, ROWS, 128), BF16),
            pltpu.SemaphoreType.DMA((len(KEYS),)),
            pltpu.SemaphoreType.DMA((len(KEYS),)),
            pltpu.SemaphoreType.DMA,
        ],
        compiler_params=pltpu.CompilerParams(collective_id=8, has_side_effects=True, vmem_limit_bytes=16 * 2**20),
        name="gather",
    )(own, pair, pltpu.with_memory_space_constraint(table, pltpu.HBM))
    return pl.pallas_call(
        write_kernel,
        out_shape=jax.ShapeDtypeStruct((LAGS, CH, 512), BF16),
        in_specs=[vmem] * 5,
        out_specs=pl.BlockSpec(memory_space=pl.ANY),
        scratch_shapes=[
            pltpu.VMEM((2, 8, NF, 256), BF16),
            pltpu.VMEM((2, CH, ROWS, 128), BF16),
            pltpu.VMEM((3, LAGS, CH, 128), BF16),
            pltpu.SemaphoreType.DMA((3 * PIECES + 8,)),
        ],
        compiler_params=pltpu.CompilerParams(vmem_limit_bytes=20 * 2**20),
        name="write",
    )(*parts)


def solution(mesh):
    return jax.shard_map(
        on_device,
        mesh=mesh,
        in_specs=(P(("grp", "dev"), None, None), P()),
        out_specs=P(None, ("grp", "dev"), None),
        check_vma=False,
    )
```
